32 devices in a mesh: rows: 8 (over z, y), grp: 4 (over x, core).
Axes of the slice: x: 2, y: 2, z: 4, core: 2. Of those that a mesh axis runs over, the one named last changes fastest.
Arguments:
- features: bfloat16 [192, 128, 2048], P('rows', None, 'grp'), may hold values from 0 to 12
- depth_weight: float32 [3, 3, 3, 2048], P(None, None, None, 'grp'), may hold values from -2 to 2
- branch_weight: bfloat16 [4, 2048, 256], P(None, 'grp'), may hold values from -0.125 to 0.125
- pool_weight: bfloat16 [2048, 256], P('grp'), may hold values from -0.125 to 0.125
- proj_weight: bfloat16 [5, 256, 256], P(None, 'grp'), may hold values from -0.15625 to 0.15625
- class_weight: bfloat16 [256, 11], replicated, may hold values from -0.375 to 0.375
- labels: int32 [192, 128], P('rows'), may hold values from 0 to 11
Outputs:
- grad_branch: float32 [4, 2048, 256], P(None, 'grp')
- grad_depth: float32 [3, 3, 3, 2048], P(None, None, None, 'grp')
- grad_pool: float32 [2048, 256], P('grp')
- grad_proj: float32 [5, 256, 256], P(None, 'grp')
- grad_class: float32 [256, 11], replicated
The draws below stay inside these ranges and needn't reach their ends.
All inputs are finite; a program needn't handle non-finite values.
Results may differ from the reference program's by a relative error of at most 0.0056.
Values may be sent and summed in bfloat16 or wider, within the bound.
A program may use at most 128 MiB of HBM per device.

```python
import math
import jax
import jax.numpy as jnp
from jax import lax

CIN = 2048
CH = 256
NCLS = 11
ROWS_DEV = 24
COLS = 128
HEIGHT = 192


def draw_features(key, part):
    key_band = jax.random.fold_in(key, 11)
    key_base = jax.random.fold_in(key, 12)
    bands = HEIGHT // ROWS_DEV
    band_scale = jnp.exp(jax.random.uniform(key_band, (bands, CIN), jnp.float32, math.log(0.5), math.log(4.0)))
    rising = jnp.exp(jnp.arange(HEIGHT, dtype=jnp.float32) * (math.log(3.0) / HEIGHT))
    scale = jnp.repeat(band_scale, ROWS_DEV, axis=0) * rising[:, None]
    base = jax.random.uniform(key_base, (HEIGHT, COLS, CIN), jnp.float32)
    return (base * scale[:, None, :]).astype(jnp.bfloat16)


def with_ends(drawn, rng, least, high):
    longest = drawn.shape.index(max(drawn.shape))
    spots = []
    for shift in (0, 1):
        where = [jax.random.randint(jax.random.fold_in(rng, axis), (), 0, length) for axis, length in enumerate(drawn.shape)]
        where[longest] = (where[longest] + shift) % drawn.shape[longest]
        spots.append(tuple(where))
    return drawn.at[spots[0]].set(least).at[spots[1]].set(high)


def shard_levels(rng, dims, shards, low, largest):
    loudness, own = 1.0, jax.random.fold_in(rng, 6)
    for axis_at, blocks in shards:
        draws = jnp.exp(jax.random.uniform(jax.random.fold_in(own, axis_at), (blocks,), jnp.float32, low / len(shards), largest / len(shards)))
        loudness = loudness * jnp.repeat(draws, dims[axis_at] // blocks).reshape([-1 if axis == axis_at else 1 for axis in range(len(dims))])
    return loudness


def scatter_about(rng, dims, scale, most, cuts=(), held_as=jnp.bfloat16):
    drawn = jax.random.normal(rng, dims, jnp.float32) * scale
    if len(cuts) > 0:
        drawn = shard_levels(rng, dims, cuts, -0.22, 0.18) * drawn
    return jnp.clip(drawn, min=-most, max=most).astype(held_as)


def setup_inputs(seed: int = 0) -> dict:
    seeds = jax.random.split(jax.random.key(seed), 8)
    features = draw_features(jax.random.fold_in(seeds[7], 71), 0)
    depth_weight = scatter_about(seeds[1], (3, 3, 3, CIN), 9 ** -0.5, 2.0, ((3, 4),), jnp.float32)
    branch_weight = scatter_about(seeds[2], (4, CIN, CH), CIN ** -0.5, 0.125, ((1, 4),))
    pool_weight = scatter_about(seeds[3], (CIN, CH), CIN ** -0.5, 0.125, ((0, 4),))
    proj_weight = scatter_about(seeds[4], (5, CH, CH), (5 * CH) ** -0.5, 0.15625, ((1, 4),))
    class_weight = scatter_about(seeds[5], (CH, NCLS), CH ** -0.5, 0.375)
    labels = with_ends(jax.random.randint(seeds[6], (HEIGHT, COLS), 0, NCLS + 1), jax.random.fold_in(seeds[6], 1), 0, NCLS).astype(jnp.int32)
    return {"features": features, "depth_weight": depth_weight, "branch_weight": branch_weight, "pool_weight": pool_weight, "proj_weight": proj_weight, "class_weight": class_weight, "labels": labels}


RATES = (6, 12, 18)
MARGIN = 18

def depth_taps(padded, weights, height, width):
    outputs = []
    for index, rate in enumerate(RATES):
        total = jnp.zeros((height, width, padded.shape[2]), jnp.float32)
        for row_tap in range(3):
            for col_tap in range(3):
                row_start = MARGIN + (row_tap - 1) * rate
                col_start = MARGIN + (col_tap - 1) * rate
                total = total + weights[index, row_tap, col_tap] * padded[row_start:row_start + height, col_start:col_start + width]
        outputs.append(total.astype(jnp.bfloat16))
    return outputs

def depth_grads(padded, backs, height, width):
    result = []
    for index, rate in enumerate(RATES):
        taps = []
        for row_tap in range(3):
            for col_tap in range(3):
                row_start = MARGIN + (row_tap - 1) * rate
                col_start = MARGIN + (col_tap - 1) * rate
                window = padded[row_start:row_start + height, col_start:col_start + width]
                taps.append(lax.optimization_barrier(jnp.sum(backs[index] * window, axis=(0, 1))))
        result.append(jnp.stack(taps).reshape(3, 3, -1))
    return jnp.stack(result)

def reference(features, depth_weight, branch_weight, pool_weight, proj_weight, class_weight, labels):
    pixels = HEIGHT * COLS
    block_size = min(256, CIN)
    f32 = jnp.float32
    pooled = lax.optimization_barrier(jnp.sum(features.astype(f32), axis=(0, 1))) / (HEIGHT * COLS)
    pre = jnp.zeros((4, pixels, CH), f32)
    for start in range(0, CIN, block_size):
        block = features[:, :, start:start + block_size]
        padded = jnp.pad(block.astype(f32), ((MARGIN, MARGIN), (MARGIN, MARGIN), (0, 0)))
        depth_out = depth_taps(padded, depth_weight[:, :, :, start:start + block_size], HEIGHT, COLS)
        inputs = [block] + depth_out
        terms = jnp.stack([jnp.dot(inputs[k].reshape(pixels, block_size), branch_weight[k, start:start + block_size], preferred_element_type=f32) for k in range(4)])
        pre = pre + terms
    pool_pre = jnp.dot(pooled, pool_weight.astype(f32), precision=lax.Precision.HIGHEST)
    branch_out = jnp.maximum(pre, 0.0).astype(jnp.bfloat16)
    pool_out = jnp.maximum(pool_pre, 0.0).astype(jnp.bfloat16)
    mixed = jnp.einsum('kpc,kcd->pd', branch_out.astype(f32), proj_weight[:4].astype(f32))
    mixed = mixed + jnp.dot(pool_out.astype(f32), proj_weight[4].astype(f32), precision=lax.Precision.HIGHEST)[None, :]
    hidden = jnp.maximum(mixed, 0.0).astype(jnp.bfloat16)
    logits = jnp.einsum('pc,ck->kp', hidden.astype(f32), class_weight.astype(f32))
    expo = jnp.exp(logits)
    soft = expo / lax.optimization_barrier(jnp.sum(expo, axis=0, keepdims=True))
    label_row = labels.reshape(pixels)
    onehot = (jnp.arange(NCLS, dtype=jnp.int32)[:, None] == label_row[None, :]).astype(f32)
    valid = (label_row < NCLS).astype(f32)
    grad_logit = ((soft - onehot) * valid[None, :] / math.sqrt(HEIGHT * COLS)).astype(jnp.bfloat16)
    grad_class = jnp.einsum('pc,kp->ck', hidden.astype(f32), grad_logit.astype(f32))
    back_hidden = jnp.einsum('ck,kp->pc', class_weight.astype(f32), grad_logit.astype(f32))
    grad_mixed = (back_hidden * (mixed > 0)).astype(jnp.bfloat16)
    col_total = lax.optimization_barrier(jnp.sum(grad_mixed.astype(f32), axis=0))
    proj_main = jnp.einsum('kpc,pd->kcd', branch_out.astype(f32), grad_mixed.astype(f32))
    proj_pool = pool_out.astype(f32)[:, None] * col_total[None, :]
    grad_proj = jnp.concatenate([proj_main, proj_pool[None]], axis=0)
    back_pre = jnp.einsum('pd,kcd->kpc', grad_mixed.astype(f32), proj_weight[:4].astype(f32))
    grad_pre = (back_pre * (pre > 0)).astype(jnp.bfloat16)
    grad_poolpre = (jnp.dot(col_total, proj_weight[4].astype(f32).T, precision=lax.Precision.HIGHEST) * (pool_pre > 0)).astype(jnp.bfloat16)
    grad_pool = pooled[:, None] * grad_poolpre.astype(f32)[None, :]
    branch_blocks = []
    depth_blocks = []
    for start in range(0, CIN, block_size):
        block = features[:, :, start:start + block_size]
        padded = jnp.pad(block.astype(f32), ((MARGIN, MARGIN), (MARGIN, MARGIN), (0, 0)))
        depth_out = depth_taps(padded, depth_weight[:, :, :, start:start + block_size], HEIGHT, COLS)
        inputs = [block] + depth_out
        branch_blocks.append(jnp.stack([jnp.einsum('pc,pd->cd', inputs[k].reshape(pixels, block_size).astype(f32), grad_pre[k].astype(f32)) for k in range(4)]))
        backs = [jnp.einsum('pd,cd->pc', grad_pre[k + 1].astype(f32), branch_weight[k + 1, start:start + block_size].astype(f32)).reshape(HEIGHT, COLS, block_size) for k in range(3)]
        depth_blocks.append(depth_grads(padded, backs, HEIGHT, COLS))
    grad_branch = jnp.concatenate(branch_blocks, axis=1)
    grad_depth = jnp.concatenate(depth_blocks, axis=3)
    return (grad_branch, grad_depth, grad_pool, grad_proj, grad_class)
```

```python
import functools
import math

import jax
import jax.numpy as jnp
from jax import lax
from jax.experimental import pallas as pl
from jax.experimental.pallas import tpu as pltpu
from jax.sharding import PartitionSpec as P

RATES = (6, 12, 18)
MARGIN = 18
MESH = pl.DeviceIdType.MESH
F32 = jnp.float32
BF16 = jnp.bfloat16
VMEM_LIMIT = 56 * 1024 * 1024


def vspec():
    return pl.BlockSpec(memory_space=pltpu.VMEM)


def remote(src, dst, send, recv, rows_at, grp_at):
    return pltpu.make_async_remote_copy(
        src_ref=src,
        dst_ref=dst,
        send_sem=send,
        recv_sem=recv,
        device_id=(rows_at, grp_at),
        device_id_type=MESH,
    )


def greet(places):
    barrier = pltpu.get_barrier_semaphore()
    for place in places:
        pl.semaphore_signal(barrier, inc=1, device_id=place, device_id_type=MESH)
    pl.semaphore_wait(barrier, len(places))


def places_of(n_rows, n_grp, me_r, me_g):
    row_peers = [(lax.rem(me_r + j, n_rows), me_g) for j in range(1, n_rows)]
    grp_peers = [(me_r, lax.rem(me_g + j, n_grp)) for j in range(1, n_grp)]
    return row_peers, grp_peers


def forward_kernel(
    n_rows,
    total_pixels,
    f,
    dw,
    weight,
    col_sum,
    pool_weight,
    proj,
    pre_out,
    proj_out,
    pool_out,
    pooled_out,
    dep,
    to_mate,
    from_mate,
    to_x,
    from_x,
    sums,
    parts,
    projs,
    big_send,
    big_recv,
    sum_send,
    sum_recv,
    part_send,
    part_recv,
    proj_send,
    proj_recv,
):
    me_r, me_g = lax.axis_index("rows"), lax.axis_index("grp")
    row_peers, grp_peers = places_of(n_rows, 4, me_r, me_g)
    greet(row_peers + grp_peers)
    height = f.shape[0] - 2 * MARGIN
    width = f.shape[1]
    channels = f.shape[2]
    hold = weight.shape[2]
    quarter_rows = height // 4
    mate = me_g + 1 - 2 * lax.rem(me_g, 2)
    x_peer = lax.rem(me_g + 2, 4)
    diag = lax.rem(mate + 2, 4)

    sums[me_r] = col_sum[...]
    sum_copies = []
    for j, (pr, pg) in enumerate(row_peers):
        copy = remote(col_sum, sums.at[me_r], sum_send.at[j], sum_recv.at[j], pr, pg)
        copy.start()
        sum_copies.append(copy)
    projs[me_g] = proj[...]
    proj_copies = []
    for j, (pr, pg) in enumerate(grp_peers):
        copy = remote(proj, projs.at[me_g], proj_send.at[j], proj_recv.at[j], pr, pg)
        copy.start()
        proj_copies.append(copy)

    column = lax.broadcasted_iota(jnp.int32, (width, 128), 0)

    def quarter(q, put):
        def pair(p, carry):
            for i in range(2):
                h = q * quarter_rows + p * 2 + i + MARGIN

                def chunk(cc, inner):
                    ch = pl.ds(pl.multiple_of(cc * 128, 128), 128)
                    mid = f[h, :, ch].astype(F32)
                    for r, rate in enumerate(RATES):
                        taps = [f[h - rate, :, ch].astype(F32), mid, f[h + rate, :, ch].astype(F32)]
                        sides = []
                        for b in range(3):
                            at = r * 9 + b
                            sides.append(
                                dw[at : at + 1, ch] * taps[0]
                                + dw[at + 3 : at + 4, ch] * taps[1]
                                + dw[at + 6 : at + 7, ch] * taps[2]
                            )
                        left = jnp.where(column >= rate, pltpu.roll(sides[0], rate, 0), 0.0)
                        right = jnp.where(
                            column < width - rate, pltpu.roll(sides[2], width - rate, 0), 0.0
                        )
                        dep[r, i * width : (i + 1) * width, ch] = (left + sides[1] + right).astype(
                            BF16
                        )
                    return inner

                lax.fori_loop(0, channels // 128, chunk, 0)
            at_row = pl.ds(pl.multiple_of(p * 2 * width, 2 * width), 2 * width)
            plain = f[pl.ds(q * quarter_rows + p * 2 + MARGIN, 2)].reshape(2 * width, channels)
            for k in range(4):
                lhs = plain if k == 0 else dep[k - 1]
                put(at_row, k, jnp.dot(lhs, weight[k], preferred_element_type=F32))
            return carry

        lax.fori_loop(0, quarter_rows // 2, pair, 0)

    def put_mate(slot):
        def put(at_row, k, value):
            to_mate[slot, at_row, k * hold : (k + 1) * hold] = value.astype(BF16)

        return put

    def put_own(at_row, k, value):
        pre_out[at_row, k * hold : (k + 1) * hold] = value

    quarter(diag, put_mate(0))
    first = remote(
        to_mate.at[0], from_mate.at[0], big_send.at[0], big_recv.at[0], me_r, mate
    )
    first.start()

    quarter(x_peer, put_own)
    first.wait()
    step = 2 * width
    count = pre_out.shape[0] // step
    x_copies = []
    for p in range(count):
        span = slice(p * step, (p + 1) * step)
        to_x[span] = (pre_out[span] + from_mate[0, span].astype(F32)).astype(BF16)
        copy = remote(
            to_x.at[span], from_x.at[span], big_send.at[2 + p], big_recv.at[2 + p], me_r, x_peer
        )
        copy.start()
        x_copies.append(copy)

    for copy in sum_copies:
        copy.wait()
    pooled = sums[0]
    for j in range(1, n_rows):
        pooled = pooled + sums[j]
    pooled = pooled / total_pixels
    pooled_out[...] = pooled
    parts[me_g] = jnp.dot(
        pooled,
        pool_weight[...].astype(F32),
        precision=lax.Precision.HIGHEST,
        preferred_element_type=F32,
    )
    part_copies = []
    for j, (pr, pg) in enumerate(grp_peers):
        copy = remote(
            parts.at[me_g], parts.at[me_g], part_send.at[j], part_recv.at[j], pr, pg
        )
        copy.start()
        part_copies.append(copy)

    quarter(mate, put_mate(1))
    second = remote(
        to_mate.at[1], from_mate.at[1], big_send.at[1], big_recv.at[1], me_r, mate
    )
    second.start()
    quarter(me_g, put_own)

    for copy in part_copies:
        copy.wait()
    pool_out[...] = parts[0] + parts[1] + parts[2] + parts[3]
    for copy in proj_copies:
        copy.wait()
    proj_out[...] = projs[...]
    second.wait()
    for p in range(count):
        span = slice(p * step, (p + 1) * step)
        x_copies[p].wait()
        pre_out[span] = (
            pre_out[span] + from_mate[1, span].astype(F32) + from_x[span].astype(F32)
        )


def gather_kernel(
    grad, proj, small, grad_out, proj_out, small_out, slots, proj_slots, small_slots,
    big_send, big_recv, proj_send, proj_recv, small_send, small_recv,
):
    me_r, me_g = lax.axis_index("rows"), lax.axis_index("grp")
    grp_peers = [(me_r, lax.rem(me_g + j, 4)) for j in range(1, 4)]
    greet(grp_peers)
    mate = me_g + 1 - 2 * lax.rem(me_g, 2)
    x_peer = lax.rem(me_g + 2, 4)
    diag = lax.rem(mate + 2, 4)
    pieces = 4
    step = grad.shape[0] // pieces
    spans = [slice(p * step, (p + 1) * step) for p in range(pieces)]
    crossing = []
    for p, span in enumerate(spans):
        copy = remote(
            grad.at[span], slots.at[1, span], big_send.at[1 + p], big_recv.at[1 + p], me_r, x_peer
        )
        copy.start()
        crossing.append(copy)
    near = remote(grad, slots.at[0], big_send.at[0], big_recv.at[0], me_r, mate)
    near.start()
    others = []
    for j, (pr, pg) in enumerate(grp_peers):
        one = remote(proj.at[pg], proj_slots.at[j], proj_send.at[j], proj_recv.at[j], pr, pg)
        two = remote(small, small_slots.at[me_g], small_send.at[j], small_recv.at[j], pr, pg)
        one.start()
        two.start()
        others += [one, two]
    small_slots[me_g] = small[...]
    grad_out[me_g] = grad[...]
    near.wait()
    grad_out[mate] = slots[0]
    passing = []
    for p, span in enumerate(spans):
        crossing[p].wait()
        copy = remote(
            slots.at[1, span],
            slots.at[2, span],
            big_send.at[1 + pieces + p],
            big_recv.at[1 + pieces + p],
            me_r,
            mate,
        )
        copy.start()
        passing.append(copy)
    grad_out[x_peer] = slots[1]
    for copy in others:
        copy.wait()
    proj_out[...] = (
        proj[me_g] + proj_slots[0] + proj_slots[1] + proj_slots[2]
    )
    small_out[...] = small_slots[0] + small_slots[1] + small_slots[2] + small_slots[3]
    for copy in passing:
        copy.wait()
    grad_out[diag] = slots[2]


def reduce_kernel(n_rows, terms, out, landed, total, gathered, s_send, s_recv, g_send, g_recv):
    me_r, me_g = lax.axis_index("rows"), lax.axis_index("grp")
    row_peers = [(lax.rem(me_r + j, n_rows), me_g) for j in range(1, n_rows)]
    greet(row_peers)
    copies = []
    for j, (pr, pg) in enumerate(row_peers):
        copy = remote(terms.at[pr], landed.at[me_r], s_send.at[j], s_recv.at[j], pr, pg)
        copy.start()
        copies.append(copy)
    landed[me_r] = terms[me_r]
    for copy in copies:
        copy.wait()
    value = landed[0].astype(F32)
    for j in range(1, n_rows):
        value = value + landed[j].astype(F32)
    total[...] = value.astype(BF16)
    copies = []
    for j, (pr, pg) in enumerate(row_peers):
        copy = remote(total, gathered.at[me_r], g_send.at[j], g_recv.at[j], pr, pg)
        copy.start()
        copies.append(copy)
    gathered[me_r] = total[...]
    for copy in copies:
        copy.wait()
    out[...] = gathered[...].astype(F32)


def params(number):
    return pltpu.CompilerParams(
        collective_id=number, has_side_effects=True, vmem_limit_bytes=VMEM_LIMIT
    )


def dma(count):
    return pltpu.SemaphoreType.DMA((count,))


def halo(block, axis, width):
    count = lax.axis_size(axis)
    forward = [(i, i + 1) for i in range(count - 1)]
    backward = [(target, source) for source, target in forward]
    low = lax.ppermute(block[block.shape[0] - width :], axis, forward)
    high = lax.ppermute(block[:width], axis, backward)
    return jnp.concatenate([low, block, high], axis=0)


def slide(block, shift):
    if shift == 0:
        return block
    width = block.shape[1]
    if shift > 0:
        return jnp.pad(block[:, : width - shift], ((0, 0), (shift, 0), (0, 0)))
    return jnp.pad(block[:, -shift:], ((0, 0), (0, -shift), (0, 0)))


def per_device(
    features, depth_weight, branch_weight, pool_weight, proj_weight, class_weight, labels
):
    height, width, channels = features.shape
    n_rows = lax.axis_size("rows")
    me_g = lax.axis_index("grp")
    hold = branch_weight.shape[2]
    own_hold = proj_weight.shape[1]
    classes = class_weight.shape[1]
    total_pixels = height * n_rows * width
    own = height * width // 4
    padded = halo(features, "rows", MARGIN)
    col_sum = jnp.sum(features.astype(F32), axis=(0, 1))
    dw = depth_weight.reshape(27, channels)

    pre, projs, pool_pre8, pooled8 = pl.pallas_call(
        functools.partial(forward_kernel, n_rows, total_pixels),
        out_shape=(
            jax.ShapeDtypeStruct((own, 4 * hold), F32),
            jax.ShapeDtypeStruct((4,) + proj_weight.shape, BF16),
            jax.ShapeDtypeStruct((8, hold), F32),
            jax.ShapeDtypeStruct((8, channels), F32),
        ),
        in_specs=[vspec()] * 6,
        out_specs=(vspec(),) * 4,
        scratch_shapes=[
            pltpu.VMEM((3, 2 * width, channels), BF16),
            pltpu.VMEM((2, own, 4 * hold), BF16),
            pltpu.VMEM((2, own, 4 * hold), BF16),
            pltpu.VMEM((own, 4 * hold), BF16),
            pltpu.VMEM((own, 4 * hold), BF16),
            pltpu.VMEM((n_rows, 8, channels), F32),
            pltpu.VMEM((4, 8, hold), F32),
            pltpu.VMEM((4,) + proj_weight.shape, BF16),
            dma(2 + height // 8),
            dma(2 + height // 8),
            dma(n_rows - 1),
            dma(n_rows - 1),
            dma(3),
            dma(3),
            dma(3),
            dma(3),
        ],
        compiler_params=params(0),
    )(
        padded,
        dw,
        branch_weight,
        jnp.broadcast_to(col_sum[None], (8, channels)),
        pool_weight,
        proj_weight,
    )
    pooled = pooled8[0]
    pool_pre = pool_pre8[0]
    proj_all = projs.transpose(1, 0, 2, 3).reshape(5, hold, hold)
    proj_main = proj_all[:4].reshape(4 * hold, hold)

    branch_out = jnp.maximum(pre, 0.0).astype(BF16)
    pool_out = jnp.maximum(pool_pre, 0.0).astype(BF16)
    pool_term = jnp.sum(pool_out.astype(F32)[:, None] * proj_all[4].astype(F32), axis=0)
    mixed = jnp.dot(branch_out, proj_main, preferred_element_type=F32) + pool_term[None, :]
    hidden = jnp.maximum(mixed, 0.0).astype(BF16)
    logits = jnp.einsum("pc,ck->kp", hidden, class_weight, preferred_element_type=F32)
    expo = jnp.exp(logits)
    soft = expo / jnp.sum(expo, axis=0, keepdims=True)
    label_row = lax.dynamic_slice_in_dim(labels.reshape(-1), me_g * own, own)
    onehot = (lax.broadcasted_iota(jnp.int32, (classes, own), 0) == label_row[None, :]).astype(F32)
    valid = (label_row < classes).astype(F32)
    grad_logit = ((soft - onehot) * valid[None, :] / math.sqrt(total_pixels)).astype(BF16)
    class_part = jnp.einsum("pc,kp->kc", hidden, grad_logit, preferred_element_type=F32)
    back_hidden = jnp.einsum("ck,kp->pc", class_weight, grad_logit, preferred_element_type=F32)
    grad_mixed = (back_hidden * (mixed > 0)).astype(BF16)
    col_part = jnp.sum(grad_mixed.astype(F32), axis=0)
    back_pre = jnp.einsum("pd,cd->pc", grad_mixed, proj_main, preferred_element_type=F32)
    grad_pre = (back_pre * (pre > 0)).astype(BF16)
    proj_part = jnp.einsum("pc,pd->cd", branch_out, grad_mixed, preferred_element_type=F32)
    proj_part = (
        proj_part.reshape(4, 4, own_hold, hold).transpose(1, 0, 2, 3).reshape(4, hold, hold)
    )
    small_rows = -(-(classes + 1) // 8) * 8
    small = jnp.concatenate(
        [class_part, col_part[None], jnp.zeros((small_rows - classes - 1, hold), F32)], axis=0
    )

    pieces = 4
    grad_all, proj_sum, small_sum = pl.pallas_call(
        gather_kernel,
        out_shape=(
            jax.ShapeDtypeStruct((4, own, 4 * hold), BF16),
            jax.ShapeDtypeStruct((hold, hold), F32),
            jax.ShapeDtypeStruct((small_rows, hold), F32),
        ),
        in_specs=[vspec()] * 3,
        out_specs=(vspec(),) * 3,
        scratch_shapes=[
            pltpu.VMEM((3, own, 4 * hold), BF16),
            pltpu.VMEM((3, hold, hold), F32),
            pltpu.VMEM((4, small_rows, hold), F32),
            dma(1 + 2 * pieces),
            dma(1 + 2 * pieces),
            dma(3),
            dma(3),
            dma(3),
            dma(3),
        ],
        compiler_params=params(1),
    )(grad_pre, proj_part, small)

    grad_all = grad_all.reshape(height, width, 4 * hold)
    pixels = height * width

    def product(shift, columns):
        window = padded[MARGIN + shift : MARGIN + shift + height].reshape(pixels, channels)
        return jnp.einsum(
            "pc,pd->cd", window, columns.reshape(pixels, -1), preferred_element_type=F32
        )

    slid = []
    for r, rate in enumerate(RATES):
        part = grad_all[:, :, (r + 1) * hold : (r + 2) * hold]
        slid.append(
            jnp.concatenate([slide(part, (b - 1) * rate) for b in range(3)], axis=2)
        )
    branch_rows = [product(0, grad_all[:, :, :hold])]
    depth_rows = []
    for r, rate in enumerate(RATES):
        branch_sum = jnp.zeros((channels, hold), F32)
        for a in range(3):
            g = product((a - 1) * rate, slid[r])
            for b in range(3):
                term = g[:, b * hold : (b + 1) * hold]
                branch_sum = branch_sum + depth_weight[r, a, b][:, None] * term
                depth_rows.append(jnp.sum(term * branch_weight[r + 1].astype(F32), axis=1))
        branch_rows.append(branch_sum)
    depth_part = jnp.stack(depth_rows)

    terms = jnp.concatenate(
        branch_rows + [depth_part.reshape(-1, hold), proj_sum, small_sum], axis=0
    ).astype(BF16)
    used = terms.shape[0]
    span = -(-used // (n_rows * 16)) * 16
    terms = jnp.pad(terms, ((0, span * n_rows - used), (0, 0))).reshape(n_rows, span, hold)
    full = pl.pallas_call(
        functools.partial(reduce_kernel, n_rows),
        out_shape=jax.ShapeDtypeStruct((n_rows, span, hold), F32),
        in_specs=[vspec()],
        out_specs=vspec(),
        scratch_shapes=[
            pltpu.VMEM((n_rows, span, hold), BF16),
            pltpu.VMEM((span, hold), BF16),
            pltpu.VMEM((n_rows, span, hold), BF16),
            dma(n_rows - 1),
            dma(n_rows - 1),
            dma(n_rows - 1),
            dma(n_rows - 1),
        ],
        compiler_params=params(2),
    )(terms)
    full = full.reshape(n_rows * span, hold)
    at = 4 * channels
    grad_branch = full[:at].reshape(4, channels, hold)
    depth_len = 27 * channels // hold
    grad_depth = full[at : at + depth_len].reshape(3, 3, 3, channels)
    at += depth_len
    proj_main_grad = full[at : at + hold].reshape(4, own_hold, hold)
    at += hold
    grad_class = full[at : at + classes].T
    col_total = full[at + classes]
    back_pool = jnp.sum(proj_all[4].astype(F32) * col_total[None, :], axis=1)
    grad_poolpre = (back_pool * (pool_pre > 0)).astype(BF16)
    grad_pool = pooled[:, None] * grad_poolpre.astype(F32)[None, :]
    own_pool = lax.dynamic_slice_in_dim(pool_out, me_g * own_hold, own_hold)
    pool_proj = own_pool.astype(F32)[:, None] * col_total[None, :]
    grad_proj = jnp.concatenate([proj_main_grad, pool_proj[None]], axis=0)
    return (grad_branch, grad_depth, grad_pool, grad_proj, grad_class)


def solution(mesh):
    return jax.shard_map(
        per_device,
        mesh=mesh,
        in_specs=(
            P("rows", None, "grp"),
            P(None, None, None, "grp"),
            P(None, "grp", None),
            P("grp", None),
            P(None, "grp", None),
            P(),
            P("rows", None),
        ),
        out_specs=(
            P(None, "grp", None),
            P(None, None, None, "grp"),
            P("grp", None),
            P(None, "grp", None),
            P(),
        ),
        check_vma=False,
    )
```

```python
import functools
import math

import jax
import jax.numpy as jnp
from jax import lax
from jax.experimental import pallas as pl
from jax.experimental.pallas import tpu as pltpu
from jax.sharding import PartitionSpec as P

RATES = (6, 12, 18)
MARGIN = 18
MESH = pl.DeviceIdType.MESH
F32 = jnp.float32
BF16 = jnp.bfloat16
VMEM_LIMIT = 56 * 1024 * 1024


def vspec():
    return pl.BlockSpec(memory_space=pltpu.VMEM)


def remote(src, dst, send, recv, rows_at, grp_at):
    return pltpu.make_async_remote_copy(
        src_ref=src,
        dst_ref=dst,
        send_sem=send,
        recv_sem=recv,
        device_id=(rows_at, grp_at),
        device_id_type=MESH,
    )


def greet(places):
    barrier = pltpu.get_barrier_semaphore()
    for place in places:
        pl.semaphore_signal(barrier, inc=1, device_id=place, device_id_type=MESH)
    pl.semaphore_wait(barrier, len(places))


def places_of(n_rows, n_grp, me_r, me_g):
    row_peers = [(lax.rem(me_r + j, n_rows), me_g) for j in range(1, n_rows)]
    grp_peers = [(me_r, lax.rem(me_g + j, n_grp)) for j in range(1, n_grp)]
    return row_peers, grp_peers


def forward_kernel(
    n_rows,
    total_pixels,
    features,
    dw,
    weight,
    col_sum,
    pool_weight,
    proj,
    pre_out,
    f,
    proj_out,
    pool_out,
    pooled_out,
    dep,
    cross,
    to_mate,
    from_mate,
    to_x,
    from_x,
    sums,
    parts,
    projs,
    local_sem,
    halo_send,
    halo_recv,
    mate_send,
    mate_recv,
    x_send,
    x_recv,
    sum_send,
    sum_recv,
    part_send,
    part_recv,
    proj_send,
    proj_recv,
):
    me_r, me_g = lax.axis_index("rows"), lax.axis_index("grp")
    row_peers, grp_peers = places_of(n_rows, 4, me_r, me_g)
    height = f.shape[0] - 2 * MARGIN
    width = f.shape[1]
    channels = f.shape[2]
    hold = weight.shape[2]
    quarter_rows = height // 4
    mate = me_g + 1 - 2 * lax.rem(me_g, 2)
    x_peer = lax.rem(me_g + 2, 4)
    diag = lax.rem(mate + 2, 4)
    greet(row_peers + grp_peers)

    after, before = lax.rem(me_r + 1, n_rows), lax.rem(me_r + n_rows - 1, n_rows)
    piece = MARGIN // 3
    up, down = [], []
    for t in range(3):
        up.append(
            remote(
                features.at[pl.ds(height - piece * (t + 1), piece)],
                f.at[pl.ds(MARGIN - piece * (t + 1), piece)],
                halo_send.at[t],
                halo_recv.at[t],
                after,
                me_g,
            )
        )
        down.append(
            remote(
                features.at[pl.ds(piece * t, piece)],
                f.at[pl.ds(MARGIN + height + piece * t, piece)],
                halo_send.at[3 + t],
                halo_recv.at[3 + t],
                before,
                me_g,
            )
        )
    middle = pltpu.make_async_copy(features, f.at[pl.ds(MARGIN, height)], local_sem)
    middle.start()
    for t in range(3):

        @pl.when(me_r < n_rows - 1)
        def _():
            up[t].start()

        @pl.when(me_r > 0)
        def _():
            down[t].start()

    @pl.when(me_r == 0)
    def _():
        f[pl.ds(0, MARGIN)] = jnp.zeros((MARGIN, width, channels), BF16)

    @pl.when(me_r == n_rows - 1)
    def _():
        f[pl.ds(MARGIN + height, MARGIN)] = jnp.zeros((MARGIN, width, channels), BF16)

    sums[me_r] = col_sum[...]
    sum_copies = []
    for j, (pr, pg) in enumerate(row_peers):
        copy = remote(col_sum, sums.at[me_r], sum_send.at[j], sum_recv.at[j], pr, pg)
        copy.start()
        sum_copies.append(copy)
    projs[me_g] = proj[...]
    proj_copies = []
    for j, (pr, pg) in enumerate(grp_peers):
        copy = remote(proj, projs.at[me_g], proj_send.at[j], proj_recv.at[j], pr, pg)
        copy.start()
        proj_copies.append(copy)

    column = lax.broadcasted_iota(jnp.int32, (width, 128), 0)

    def quarter(q, k, put):
        def pair(p, carry):
            first_row = q * quarter_rows + p * 2 + MARGIN
            if k == 0:
                lhs = f[pl.ds(first_row, 2)].reshape(2 * width, channels)
            else:
                rate = RATES[k - 1]

                def chunk(cc, inner):
                    ch = pl.ds(pl.multiple_of(cc * 128, 128), 128)
                    for i in range(2):
                        h = first_row + i
                        taps = [f[h + (a - 1) * rate, :, ch].astype(F32) for a in range(3)]
                        sides = []
                        for b in range(3):
                            at = (k - 1) * 9 + b
                            sides.append(
                                dw[at : at + 1, ch] * taps[0]
                                + dw[at + 3 : at + 4, ch] * taps[1]
                                + dw[at + 6 : at + 7, ch] * taps[2]
                            )
                        left = jnp.where(column >= rate, pltpu.roll(sides[0], rate, 0), 0.0)
                        right = jnp.where(
                            column < width - rate, pltpu.roll(sides[2], width - rate, 0), 0.0
                        )
                        dep[i * width : (i + 1) * width, ch] = (left + sides[1] + right).astype(
                            BF16
                        )
                    return inner

                lax.fori_loop(0, channels // 128, chunk, 0)
                lhs = dep[...]
            at_row = pl.ds(pl.multiple_of(p * 2 * width, 2 * width), 2 * width)
            put(at_row, jnp.dot(lhs, weight[k], preferred_element_type=F32))
            return carry

        lax.fori_loop(0, quarter_rows // 2, pair, 0)

    seconds, crossings = [], []

    def branch(k):
        def put_mate(slot):
            def put(at_row, value):
                to_mate[k, slot, at_row] = value.astype(BF16)

            return put

        def put_cross(at_row, value):
            cross[at_row] = value

        def put_own(at_row, value):
            pre_out[at_row, k * hold : (k + 1) * hold] = value

        def to_core(slot):
            copy = remote(
                to_mate.at[k, slot],
                from_mate.at[k, slot],
                mate_send.at[2 * k + slot],
                mate_recv.at[2 * k + slot],
                me_r,
                mate,
            )
            copy.start()
            return copy

        quarter(diag, k, put_mate(0))
        first = to_core(0)
        quarter(x_peer, k, put_cross)
        first.wait()
        to_x[k] = (cross[...] + from_mate[k, 0].astype(F32)).astype(BF16)
        crossing = remote(
            to_x.at[k], from_x.at[k], x_send.at[k], x_recv.at[k], me_r, x_peer
        )
        crossing.start()
        crossings.append(crossing)
        quarter(mate, k, put_mate(1))
        seconds.append(to_core(1))
        quarter(me_g, k, put_own)

    middle.wait()
    branch(0)
    for copy in sum_copies:
        copy.wait()
    pooled = sums[0]
    for j in range(1, n_rows):
        pooled = pooled + sums[j]
    pooled = pooled / total_pixels
    pooled_out[...] = pooled
    parts[me_g] = jnp.dot(
        pooled,
        pool_weight[...].astype(F32),
        precision=lax.Precision.HIGHEST,
        preferred_element_type=F32,
    )
    part_copies = []
    for j, (pr, pg) in enumerate(grp_peers):
        copy = remote(
            parts.at[me_g], parts.at[me_g], part_send.at[j], part_recv.at[j], pr, pg
        )
        copy.start()
        part_copies.append(copy)
    for copy in part_copies:
        copy.wait()
    pool_out[...] = parts[0] + parts[1] + parts[2] + parts[3]
    for copy in proj_copies:
        copy.wait()
    proj_out[...] = projs[...]

    for k in range(1, 4):

        @pl.when(me_r > 0)
        def _():
            up[k - 1].wait_recv()

        @pl.when(me_r < n_rows - 1)
        def _():
            down[k - 1].wait_recv()

        branch(k)

    for k in range(4):
        seconds[k].wait()
        crossings[k].wait()
        span = slice(k * hold, (k + 1) * hold)
        pre_out[:, span] = (
            pre_out[:, span] + from_mate[k, 1].astype(F32) + from_x[k].astype(F32)
        )
    for t in range(3):

        @pl.when(me_r < n_rows - 1)
        def _():
            up[t].wait_send()

        @pl.when(me_r > 0)
        def _():
            down[t].wait_send()


def gather_kernel(
    grad, proj, small, grad_out, proj_out, small_out, slots, proj_slots, small_slots,
    big_send, big_recv, proj_send, proj_recv, small_send, small_recv,
):
    me_r, me_g = lax.axis_index("rows"), lax.axis_index("grp")
    grp_peers = [(me_r, lax.rem(me_g + j, 4)) for j in range(1, 4)]
    greet(grp_peers)
    mate = me_g + 1 - 2 * lax.rem(me_g, 2)
    x_peer = lax.rem(me_g + 2, 4)
    diag = lax.rem(mate + 2, 4)
    pieces = 4
    step = grad.shape[0] // pieces
    spans = [slice(p * step, (p + 1) * step) for p in range(pieces)]
    crossing = []
    for p, span in enumerate(spans):
        copy = remote(
            grad.at[span], slots.at[1, span], big_send.at[1 + p], big_recv.at[1 + p], me_r, x_peer
        )
        copy.start()
        crossing.append(copy)
    near = remote(grad, slots.at[0], big_send.at[0], big_recv.at[0], me_r, mate)
    near.start()
    others = []
    for j, (pr, pg) in enumerate(grp_peers):
        one = remote(proj.at[pg], proj_slots.at[j], proj_send.at[j], proj_recv.at[j], pr, pg)
        two = remote(small, small_slots.at[me_g], small_send.at[j], small_recv.at[j], pr, pg)
        one.start()
        two.start()
        others += [one, two]
    small_slots[me_g] = small[...]
    grad_out[me_g] = grad[...]
    near.wait()
    grad_out[mate] = slots[0]
    passing = []
    for p, span in enumerate(spans):
        crossing[p].wait()
        copy = remote(
            slots.at[1, span],
            slots.at[2, span],
            big_send.at[1 + pieces + p],
            big_recv.at[1 + pieces + p],
            me_r,
            mate,
        )
        copy.start()
        passing.append(copy)
    grad_out[x_peer] = slots[1]
    for copy in others:
        copy.wait()
    proj_out[...] = (
        proj[me_g] + proj_slots[0] + proj_slots[1] + proj_slots[2]
    )
    small_out[...] = small_slots[0] + small_slots[1] + small_slots[2] + small_slots[3]
    for copy in passing:
        copy.wait()
    grad_out[diag] = slots[2]


def reduce_kernel(n_rows, terms, out, landed, total, gathered, s_send, s_recv, g_send, g_recv):
    me_r, me_g = lax.axis_index("rows"), lax.axis_index("grp")
    row_peers = [(lax.rem(me_r + j, n_rows), me_g) for j in range(1, n_rows)]
    greet(row_peers)
    copies = []
    for j, (pr, pg) in enumerate(row_peers):
        copy = remote(terms.at[pr], landed.at[me_r], s_send.at[j], s_recv.at[j], pr, pg)
        copy.start()
        copies.append(copy)
    landed[me_r] = terms[me_r]
    for copy in copies:
        copy.wait()
    value = landed[0].astype(F32)
    for j in range(1, n_rows):
        value = value + landed[j].astype(F32)
    total[...] = value.astype(BF16)
    copies = []
    for j, (pr, pg) in enumerate(row_peers):
        copy = remote(total, gathered.at[me_r], g_send.at[j], g_recv.at[j], pr, pg)
        copy.start()
        copies.append(copy)
    gathered[me_r] = total[...]
    for copy in copies:
        copy.wait()
    out[...] = gathered[...].astype(F32)


def params(number):
    return pltpu.CompilerParams(
        collective_id=number, has_side_effects=True, vmem_limit_bytes=VMEM_LIMIT
    )


def dma(count):
    return pltpu.SemaphoreType.DMA((count,))


def slide(block, shift):
    if shift == 0:
        return block
    width = block.shape[1]
    if shift > 0:
        return jnp.pad(block[:, : width - shift], ((0, 0), (shift, 0), (0, 0)))
    return jnp.pad(block[:, -shift:], ((0, 0), (0, -shift), (0, 0)))


def per_device(
    features, depth_weight, branch_weight, pool_weight, proj_weight, class_weight, labels
):
    height, width, channels = features.shape
    n_rows = lax.axis_size("rows")
    me_g = lax.axis_index("grp")
    hold = branch_weight.shape[2]
    own_hold = proj_weight.shape[1]
    classes = class_weight.shape[1]
    total_pixels = height * n_rows * width
    own = height * width // 4
    col_sum = jnp.sum(features.astype(F32), axis=(0, 1))
    dw = depth_weight.reshape(27, channels)

    pre, padded, projs, pool_pre8, pooled8 = pl.pallas_call(
        functools.partial(forward_kernel, n_rows, total_pixels),
        out_shape=(
            jax.ShapeDtypeStruct((own, 4 * hold), F32),
            jax.ShapeDtypeStruct((height + 2 * MARGIN, width, channels), BF16),
            jax.ShapeDtypeStruct((4,) + proj_weight.shape, BF16),
            jax.ShapeDtypeStruct((8, hold), F32),
            jax.ShapeDtypeStruct((8, channels), F32),
        ),
        in_specs=[pl.BlockSpec(memory_space=pl.ANY)] + [vspec()] * 5,
        out_specs=(vspec(),) * 5,
        scratch_shapes=[
            pltpu.VMEM((2 * width, channels), BF16),
            pltpu.VMEM((own, hold), F32),
            pltpu.VMEM((4, 2, own, hold), BF16),
            pltpu.VMEM((4, 2, own, hold), BF16),
            pltpu.VMEM((4, own, hold), BF16),
            pltpu.VMEM((4, own, hold), BF16),
            pltpu.VMEM((n_rows, 8, channels), F32),
            pltpu.VMEM((4, 8, hold), F32),
            pltpu.VMEM((4,) + proj_weight.shape, BF16),
            pltpu.SemaphoreType.DMA,
            dma(6),
            dma(6),
            dma(8),
            dma(8),
            dma(4),
            dma(4),
            dma(n_rows - 1),
            dma(n_rows - 1),
            dma(3),
            dma(3),
            dma(3),
            dma(3),
        ],
        compiler_params=params(0),
    )(
        features,
        dw,
        branch_weight,
        jnp.broadcast_to(col_sum[None], (8, channels)),
        pool_weight,
        proj_weight,
    )
    pooled = pooled8[0]
    pool_pre = pool_pre8[0]
    proj_all = projs.transpose(1, 0, 2, 3).reshape(5, hold, hold)
    proj_main = proj_all[:4].reshape(4 * hold, hold)

    branch_out = jnp.maximum(pre, 0.0).astype(BF16)
    pool_out = jnp.maximum(pool_pre, 0.0).astype(BF16)
    pool_term = jnp.sum(pool_out.astype(F32)[:, None] * proj_all[4].astype(F32), axis=0)
    mixed = jnp.dot(branch_out, proj_main, preferred_element_type=F32) + pool_term[None, :]
    hidden = jnp.maximum(mixed, 0.0).astype(BF16)
    logits = jnp.einsum("pc,ck->kp", hidden, class_weight, preferred_element_type=F32)
    expo = jnp.exp(logits)
    soft = expo / jnp.sum(expo, axis=0, keepdims=True)
    label_row = lax.dynamic_slice_in_dim(labels.reshape(-1), me_g * own, own)
    onehot = (lax.broadcasted_iota(jnp.int32, (classes, own), 0) == label_row[None, :]).astype(F32)
    valid = (label_row < classes).astype(F32)
    grad_logit = ((soft - onehot) * valid[None, :] / math.sqrt(total_pixels)).astype(BF16)
    class_part = jnp.einsum("pc,kp->kc", hidden, grad_logit, preferred_element_type=F32)
    back_hidden = jnp.einsum("ck,kp->pc", class_weight, grad_logit, preferred_element_type=F32)
    grad_mixed = (back_hidden * (mixed > 0)).astype(BF16)
    col_part = jnp.sum(grad_mixed.astype(F32), axis=0)
    back_pre = jnp.einsum("pd,cd->pc", grad_mixed, proj_main, preferred_element_type=F32)
    grad_pre = (back_pre * (pre > 0)).astype(BF16)
    proj_part = jnp.einsum("pc,pd->cd", branch_out, grad_mixed, preferred_element_type=F32)
    proj_part = (
        proj_part.reshape(4, 4, own_hold, hold).transpose(1, 0, 2, 3).reshape(4, hold, hold)
    )
    small_rows = -(-(classes + 1) // 8) * 8
    small = jnp.concatenate(
        [class_part, col_part[None], jnp.zeros((small_rows - classes - 1, hold), F32)], axis=0
    )

    pieces = 4
    grad_all, proj_sum, small_sum = pl.pallas_call(
        gather_kernel,
        out_shape=(
            jax.ShapeDtypeStruct((4, own, 4 * hold), BF16),
            jax.ShapeDtypeStruct((hold, hold), F32),
            jax.ShapeDtypeStruct((small_rows, hold), F32),
        ),
        in_specs=[vspec()] * 3,
        out_specs=(vspec(),) * 3,
        scratch_shapes=[
            pltpu.VMEM((3, own, 4 * hold), BF16),
            pltpu.VMEM((3, hold, hold), F32),
            pltpu.VMEM((4, small_rows, hold), F32),
            dma(1 + 2 * pieces),
            dma(1 + 2 * pieces),
            dma(3),
            dma(3),
            dma(3),
            dma(3),
        ],
        compiler_params=params(1),
    )(grad_pre, proj_part, small)

    grad_all = grad_all.reshape(height, width, 4 * hold)
    pixels = height * width

    def product(shift, columns):
        window = padded[MARGIN + shift : MARGIN + shift + height].reshape(pixels, channels)
        return jnp.einsum(
            "pc,pd->cd", window, columns.reshape(pixels, -1), preferred_element_type=F32
        )

    slid = []
    for r, rate in enumerate(RATES):
        part = grad_all[:, :, (r + 1) * hold : (r + 2) * hold]
        slid.append(
            jnp.concatenate([slide(part, (b - 1) * rate) for b in range(3)], axis=2)
        )
    branch_rows = [product(0, grad_all[:, :, :hold])]
    depth_rows = []
    for r, rate in enumerate(RATES):
        branch_sum = jnp.zeros((channels, hold), F32)
        for a in range(3):
            g = product((a - 1) * rate, slid[r])
            for b in range(3):
                term = g[:, b * hold : (b + 1) * hold]
                branch_sum = branch_sum + depth_weight[r, a, b][:, None] * term
                depth_rows.append(jnp.sum(term * branch_weight[r + 1].astype(F32), axis=1))
        branch_rows.append(branch_sum)
    depth_part = jnp.stack(depth_rows)

    terms = jnp.concatenate(
        branch_rows + [depth_part.reshape(-1, hold), proj_sum, small_sum], axis=0
    ).astype(BF16)
    used = terms.shape[0]
    span = -(-used // (n_rows * 16)) * 16
    terms = jnp.pad(terms, ((0, span * n_rows - used), (0, 0))).reshape(n_rows, span, hold)
    full = pl.pallas_call(
        functools.partial(reduce_kernel, n_rows),
        out_shape=jax.ShapeDtypeStruct((n_rows, span, hold), F32),
        in_specs=[vspec()],
        out_specs=vspec(),
        scratch_shapes=[
            pltpu.VMEM((n_rows, span, hold), BF16),
            pltpu.VMEM((span, hold), BF16),
            pltpu.VMEM((n_rows, span, hold), BF16),
            dma(n_rows - 1),
            dma(n_rows - 1),
            dma(n_rows - 1),
            dma(n_rows - 1),
        ],
        compiler_params=params(2),
    )(terms)
    full = full.reshape(n_rows * span, hold)
    at = 4 * channels
    grad_branch = full[:at].reshape(4, channels, hold)
    depth_len = 27 * channels // hold
    grad_depth = full[at : at + depth_len].reshape(3, 3, 3, channels)
    at += depth_len
    proj_main_grad = full[at : at + hold].reshape(4, own_hold, hold)
    at += hold
    grad_class = full[at : at + classes].T
    col_total = full[at + classes]
    back_pool = jnp.sum(proj_all[4].astype(F32) * col_total[None, :], axis=1)
    grad_poolpre = (back_pool * (pool_pre > 0)).astype(BF16)
    grad_pool = pooled[:, None] * grad_poolpre.astype(F32)[None, :]
    own_pool = lax.dynamic_slice_in_dim(pool_out, me_g * own_hold, own_hold)
    pool_proj = own_pool.astype(F32)[:, None] * col_total[None, :]
    grad_proj = jnp.concatenate([proj_main_grad, pool_proj[None]], axis=0)
    return (grad_branch, grad_depth, grad_pool, grad_proj, grad_class)


def solution(mesh):
    return jax.shard_map(
        per_device,
        mesh=mesh,
        in_specs=(
            P("rows", None, "grp"),
            P(None, None, None, "grp"),
            P(None, "grp", None),
            P("grp", None),
            P(None, "grp", None),
            P(),
            P("rows", None),
        ),
        out_specs=(
            P(None, "grp", None),
            P(None, None, None, "grp"),
            P("grp", None),
            P(None, "grp", None),
            P(),
        ),
        check_vma=False,
    )
```

```python
import functools
import math

import jax
import jax.numpy as jnp
from jax import lax
from jax.experimental import pallas as pl
from jax.experimental.pallas import tpu as pltpu
from jax.sharding import PartitionSpec as P

RATES = (6, 12, 18)
MARGIN = 18
MESH = pl.DeviceIdType.MESH
F32 = jnp.float32
BF16 = jnp.bfloat16
VMEM_LIMIT = 56 * 1024 * 1024


def vspec():
    return pl.BlockSpec(memory_space=pltpu.VMEM)


def remote(src, dst, send, recv, rows_at, grp_at):
    return pltpu.make_async_remote_copy(
        src_ref=src,
        dst_ref=dst,
        send_sem=send,
        recv_sem=recv,
        device_id=(rows_at, grp_at),
        device_id_type=MESH,
    )


def greet(places):
    barrier = pltpu.get_barrier_semaphore()
    for place in places:
        pl.semaphore_signal(barrier, inc=1, device_id=place, device_id_type=MESH)
    pl.semaphore_wait(barrier, len(places))


def places_of(n_rows, n_grp, me_r, me_g):
    row_peers = [(lax.rem(me_r + j, n_rows), me_g) for j in range(1, n_rows)]
    grp_peers = [(me_r, lax.rem(me_g + j, n_grp)) for j in range(1, n_grp)]
    return row_peers, grp_peers


def forward_kernel(
    n_rows,
    total_pixels,
    features,
    dw,
    weight,
    col_sum,
    pool_weight,
    proj,
    pre_out,
    f,
    proj_out,
    pool_out,
    pooled_out,
    dep,
    cross,
    to_mate,
    from_mate,
    to_x,
    from_x,
    sums,
    parts,
    projs,
    local_sem,
    halo_send,
    halo_recv,
    mate_send,
    mate_recv,
    x_send,
    x_recv,
    sum_send,
    sum_recv,
    part_send,
    part_recv,
    proj_send,
    proj_recv,
):
    me_r, me_g = lax.axis_index("rows"), lax.axis_index("grp")
    row_peers, grp_peers = places_of(n_rows, 4, me_r, me_g)
    height = f.shape[0] - 2 * MARGIN
    width = f.shape[1]
    channels = f.shape[2]
    hold = weight.shape[2]
    quarter_rows = height // 4
    mate = me_g + 1 - 2 * lax.rem(me_g, 2)
    x_peer = lax.rem(me_g + 2, 4)
    diag = lax.rem(mate + 2, 4)
    greet(row_peers + grp_peers)

    after, before = lax.rem(me_r + 1, n_rows), lax.rem(me_r + n_rows - 1, n_rows)
    piece = MARGIN // 3
    up, down = [], []
    for t in range(3):
        up.append(
            remote(
                features.at[pl.ds(height - piece * (t + 1), piece)],
                f.at[pl.ds(MARGIN - piece * (t + 1), piece)],
                halo_send.at[t],
                halo_recv.at[t],
                after,
                me_g,
            )
        )
        down.append(
            remote(
                features.at[pl.ds(piece * t, piece)],
                f.at[pl.ds(MARGIN + height + piece * t, piece)],
                halo_send.at[3 + t],
                halo_recv.at[3 + t],
                before,
                me_g,
            )
        )
    middle = pltpu.make_async_copy(features, f.at[pl.ds(MARGIN, height)], local_sem)
    middle.start()
    for t in range(3):

        @pl.when(me_r < n_rows - 1)
        def _():
            up[t].start()

        @pl.when(me_r > 0)
        def _():
            down[t].start()

    @pl.when(me_r == 0)
    def _():
        f[pl.ds(0, MARGIN)] = jnp.zeros((MARGIN, width, channels), BF16)

    @pl.when(me_r == n_rows - 1)
    def _():
        f[pl.ds(MARGIN + height, MARGIN)] = jnp.zeros((MARGIN, width, channels), BF16)

    sums[me_r] = col_sum[...]
    sum_copies = []
    for j, (pr, pg) in enumerate(row_peers):
        copy = remote(col_sum, sums.at[me_r], sum_send.at[j], sum_recv.at[j], pr, pg)
        copy.start()
        sum_copies.append(copy)
    projs[me_g] = proj[...]
    proj_copies = []
    for j, (pr, pg) in enumerate(grp_peers):
        copy = remote(proj, projs.at[me_g], proj_send.at[j], proj_recv.at[j], pr, pg)
        copy.start()
        proj_copies.append(copy)

    column = lax.broadcasted_iota(jnp.int32, (width, 128), 0)

    def quarter(q, k, put):
        def pair(p, carry):
            first_row = q * quarter_rows + p * 2 + MARGIN
            if k == 0:
                lhs = f[pl.ds(first_row, 2)].reshape(2 * width, channels)
            else:
                rate = RATES[k - 1]

                def chunk(cc, inner):
                    ch = pl.ds(pl.multiple_of(cc * 128, 128), 128)
                    for i in range(2):
                        h = first_row + i
                        taps = [f[h + (a - 1) * rate, :, ch].astype(F32) for a in range(3)]
                        sides = []
                        for b in range(3):
                            at = (k - 1) * 9 + b
                            sides.append(
                                dw[at : at + 1, ch] * taps[0]
                                + dw[at + 3 : at + 4, ch] * taps[1]
                                + dw[at + 6 : at + 7, ch] * taps[2]
                            )
                        left = jnp.where(column >= rate, pltpu.roll(sides[0], rate, 0), 0.0)
                        right = jnp.where(
                            column < width - rate, pltpu.roll(sides[2], width - rate, 0), 0.0
                        )
                        dep[i * width : (i + 1) * width, ch] = (left + sides[1] + right).astype(
                            BF16
                        )
                    return inner

                lax.fori_loop(0, channels // 128, chunk, 0)
                lhs = dep[...]
            at_row = pl.ds(pl.multiple_of(p * 2 * width, 2 * width), 2 * width)
            put(at_row, jnp.dot(lhs, weight[k], preferred_element_type=F32))
            return carry

        lax.fori_loop(0, quarter_rows // 2, pair, 0)

    seconds, crossings = [], []

    def branch(k):
        def put_mate(slot):
            def put(at_row, value):
                to_mate[k, slot, at_row] = value.astype(BF16)

            return put

        def put_cross(at_row, value):
            cross[at_row] = value

        def put_own(at_row, value):
            pre_out[at_row, k * hold : (k + 1) * hold] = value

        def to_core(slot):
            copy = remote(
                to_mate.at[k, slot],
                from_mate.at[k, slot],
                mate_send.at[2 * k + slot],
                mate_recv.at[2 * k + slot],
                me_r,
                mate,
            )
            copy.start()
            return copy

        quarter(diag, k, put_mate(0))
        first = to_core(0)
        quarter(x_peer, k, put_cross)
        first.wait()
        to_x[k] = (cross[...] + from_mate[k, 0].astype(F32)).astype(BF16)
        crossing = remote(
            to_x.at[k], from_x.at[k], x_send.at[k], x_recv.at[k], me_r, x_peer
        )
        crossing.start()
        crossings.append(crossing)
        quarter(mate, k, put_mate(1))
        seconds.append(to_core(1))
        quarter(me_g, k, put_own)

    middle.wait()
    branch(0)
    for copy in sum_copies:
        copy.wait()
    pooled = sums[0]
    for j in range(1, n_rows):
        pooled = pooled + sums[j]
    pooled = pooled / total_pixels
    pooled_out[...] = pooled
    parts[me_g] = jnp.dot(
        pooled,
        pool_weight[...].astype(F32),
        precision=lax.Precision.HIGHEST,
        preferred_element_type=F32,
    )
    part_copies = []
    for j, (pr, pg) in enumerate(grp_peers):
        copy = remote(
            parts.at[me_g], parts.at[me_g], part_send.at[j], part_recv.at[j], pr, pg
        )
        copy.start()
        part_copies.append(copy)
    for copy in part_copies:
        copy.wait()
    pool_out[...] = parts[0] + parts[1] + parts[2] + parts[3]
    for copy in proj_copies:
        copy.wait()
    proj_out[...] = projs[...]

    for k in range(1, 4):

        @pl.when(me_r > 0)
        def _():
            up[k - 1].wait_recv()

        @pl.when(me_r < n_rows - 1)
        def _():
            down[k - 1].wait_recv()

        branch(k)

    for k in range(4):
        seconds[k].wait()
        crossings[k].wait()
        span = slice(k * hold, (k + 1) * hold)
        pre_out[:, span] = (
            pre_out[:, span] + from_mate[k, 1].astype(F32) + from_x[k].astype(F32)
        )
    for t in range(3):

        @pl.when(me_r < n_rows - 1)
        def _():
            up[t].wait_send()

        @pl.when(me_r > 0)
        def _():
            down[t].wait_send()


def backward_kernel(
    n_rows,
    grad,
    proj,
    small,
    f,
    dw,
    weight_t,
    branch_out,
    rest_out,
    grads,
    acc,
    depth,
    terms,
    rest,
    landed,
    landed_rest,
    total,
    total_rest,
    gathered,
    gathered_rest,
    proj_slots,
    small_slots,
    big_send,
    big_recv,
    proj_send,
    proj_recv,
    small_send,
    small_recv,
    s_send,
    s_recv,
    g_send,
    g_recv,
):
    me_r, me_g = lax.axis_index("rows"), lax.axis_index("grp")
    row_peers, grp_peers = places_of(n_rows, 4, me_r, me_g)
    greet(row_peers + grp_peers)
    mate = me_g + 1 - 2 * lax.rem(me_g, 2)
    x_peer = lax.rem(me_g + 2, 4)
    height = f.shape[0] - 2 * MARGIN
    width, channels = f.shape[1], f.shape[2]
    hold = grad.shape[1]
    own = grad.shape[2]
    halves = channels // 256

    crossing, near = [], []
    for k in range(4):
        one = remote(
            grad.at[k], grads.at[me_g, k], big_send.at[k], big_recv.at[k], me_r, x_peer
        )
        two = remote(
            grad.at[k], grads.at[me_g, k], big_send.at[4 + k], big_recv.at[4 + k], me_r, mate
        )
        one.start()
        two.start()
        crossing.append(one)
        near.append(two)
    others = []
    for j, (pr, pg) in enumerate(grp_peers):
        one = remote(proj.at[pg], proj_slots.at[me_g], proj_send.at[j], proj_recv.at[j], pr, pg)
        two = remote(small, small_slots.at[me_g], small_send.at[j], small_recv.at[j], pr, pg)
        one.start()
        two.start()
        others += [one, two]
    proj_slots[me_g] = proj[me_g]
    small_slots[me_g] = small[...]
    grads[me_g] = grad[...]
    depth[...] = jnp.zeros(depth.shape, F32)
    lane = lax.broadcasted_iota(jnp.int32, (hold, width), 1)
    pairs = own // (2 * width)

    def products(k):
        acc[...] = jnp.zeros(acc.shape, F32)

        def step(p, carry):
            q, within = p // pairs, lax.rem(p, pairs)
            at = pl.ds(pl.multiple_of(within * 2 * width, 2 * width), 2 * width)
            block = grads[q, k, :, at]
            if k == 0:
                rows = f[pl.ds(p * 2 + MARGIN, 2)].reshape(2 * width, channels)
                acc[0, :hold] += jnp.dot(block, rows, preferred_element_type=F32)
                return carry
            rate = RATES[k - 1]
            wide = block.astype(F32)
            lefts, rights = [], []
            for i in range(2):
                x = wide[:, i * width : (i + 1) * width]
                lefts.append(
                    jnp.where(lane < width - rate, pltpu.roll(x, width - rate, 1), 0.0)
                )
                rights.append(jnp.where(lane >= rate, pltpu.roll(x, rate, 1), 0.0))
            left = jnp.concatenate(lefts, axis=1).astype(BF16)
            right = jnp.concatenate(rights, axis=1).astype(BF16)
            for a in range(3):
                rows = f[pl.ds(p * 2 + MARGIN + (a - 1) * rate, 2)].reshape(2 * width, channels)
                for b, lhs in enumerate((left, block, right)):
                    acc[a, b * hold : (b + 1) * hold] += jnp.dot(
                        lhs, rows, preferred_element_type=F32
                    )
            return carry

        lax.fori_loop(0, height // 2, step, 0)

    def spread(unit, source, target):
        copies = []
        for j, (pr, pg) in enumerate(row_peers):
            at = unit * (n_rows - 1) + j
            copy = remote(source(pr), target, s_send.at[at], s_recv.at[at], pr, pg)
            copy.start()
            copies.append(copy)
        return copies

    def share(unit, source, target):
        copies = []
        for j, (pr, pg) in enumerate(row_peers):
            at = unit * (n_rows - 1) + j
            copy = remote(source, target, g_send.at[at], g_recv.at[at], pr, pg)
            copy.start()
            copies.append(copy)
        return copies

    def add_up(parts):
        value = parts[0].astype(F32)
        for j in range(1, n_rows):
            value = value + parts[j].astype(F32)
        return value.astype(BF16)

    spreading, sharing = [], []

    def finish(k):
        for copy in spreading[k]:
            copy.wait()
        total[k] = add_up([landed[k, j] for j in range(n_rows)])
        gathered[k, me_r] = total[k]
        sharing.append(share(k, total.at[k], gathered.at[k, me_r]))

    span = terms.shape[2]
    passing = []
    for k in range(4):
        crossing[k].wait()
        copy = remote(
            grads.at[x_peer, k],
            grads.at[x_peer, k],
            big_send.at[8 + k],
            big_recv.at[8 + k],
            me_r,
            mate,
        )
        copy.start()
        passing.append(copy)
        near[k].wait()
        copy.wait()
        products(k)
        if k == 0:
            value = acc[0, :hold]
        else:
            value = jnp.zeros((hold, channels), F32)
            for a in range(3):
                for b in range(3):
                    at = (k - 1) * 9 + a * 3 + b
                    term = acc[a, b * hold : (b + 1) * hold]
                    value = value + dw[at : at + 1, :] * term
                    depth[at : at + 1, :] = jnp.sum(
                        weight_t[k - 1].astype(F32) * term, axis=0, keepdims=True
                    )
        flat = jnp.concatenate(
            [value[:, c * 256 : (c + 1) * 256] for c in range(halves)], axis=0
        ).astype(BF16)
        terms[k] = flat.reshape(n_rows, span, 256)
        landed[k, me_r] = terms[k, me_r]
        spreading.append(
            spread(k, lambda pr, k=k: terms.at[k, pr], landed.at[k, me_r])
        )
        if k > 0:
            finish(k - 1)

    for copy in others:
        copy.wait()
    lines = [depth[:, c * 256 : (c + 1) * 256] for c in range(halves)]
    lines.append(proj_slots[0] + proj_slots[1] + proj_slots[2] + proj_slots[3])
    lines.append(small_slots[0] + small_slots[1] + small_slots[2] + small_slots[3])
    flat = jnp.concatenate(lines, axis=0)
    spare = rest.shape[0] * rest.shape[1] - flat.shape[0]
    flat = jnp.concatenate([flat, jnp.zeros((spare, 256), F32)], axis=0).astype(BF16)
    rest[...] = flat.reshape(rest.shape)
    landed_rest[me_r] = rest[me_r]
    last = spread(4, lambda pr: rest.at[pr], landed_rest.at[me_r])
    finish(3)
    for copy in last:
        copy.wait()
    total_rest[...] = add_up([landed_rest[j] for j in range(n_rows)])
    gathered_rest[me_r] = total_rest[...]
    last = share(4, total_rest, gathered_rest.at[me_r])
    for k in range(4):
        for copy in sharing[k]:
            copy.wait()
        branch_out[k] = gathered[k].astype(F32)
    for copy in last:
        copy.wait()
    rest_out[...] = gathered_rest[...].astype(F32)


def params(number):
    return pltpu.CompilerParams(
        collective_id=number, has_side_effects=True, vmem_limit_bytes=VMEM_LIMIT
    )


def dma(count):
    return pltpu.SemaphoreType.DMA((count,))


def per_device(
    features, depth_weight, branch_weight, pool_weight, proj_weight, class_weight, labels
):
    height, width, channels = features.shape
    n_rows = lax.axis_size("rows")
    me_g = lax.axis_index("grp")
    hold = branch_weight.shape[2]
    own_hold = proj_weight.shape[1]
    classes = class_weight.shape[1]
    total_pixels = height * n_rows * width
    own = height * width // 4
    col_sum = jnp.sum(features.astype(F32), axis=(0, 1))
    dw = depth_weight.reshape(27, channels)

    pre, padded, projs, pool_pre8, pooled8 = pl.pallas_call(
        functools.partial(forward_kernel, n_rows, total_pixels),
        out_shape=(
            jax.ShapeDtypeStruct((own, 4 * hold), F32),
            jax.ShapeDtypeStruct((height + 2 * MARGIN, width, channels), BF16),
            jax.ShapeDtypeStruct((4,) + proj_weight.shape, BF16),
            jax.ShapeDtypeStruct((8, hold), F32),
            jax.ShapeDtypeStruct((8, channels), F32),
        ),
        in_specs=[pl.BlockSpec(memory_space=pl.ANY)] + [vspec()] * 5,
        out_specs=(vspec(),) * 5,
        scratch_shapes=[
            pltpu.VMEM((2 * width, channels), BF16),
            pltpu.VMEM((own, hold), F32),
            pltpu.VMEM((4, 2, own, hold), BF16),
            pltpu.VMEM((4, 2, own, hold), BF16),
            pltpu.VMEM((4, own, hold), BF16),
            pltpu.VMEM((4, own, hold), BF16),
            pltpu.VMEM((n_rows, 8, channels), F32),
            pltpu.VMEM((4, 8, hold), F32),
            pltpu.VMEM((4,) + proj_weight.shape, BF16),
            pltpu.SemaphoreType.DMA,
            dma(6),
            dma(6),
            dma(8),
            dma(8),
            dma(4),
            dma(4),
            dma(n_rows - 1),
            dma(n_rows - 1),
            dma(3),
            dma(3),
            dma(3),
            dma(3),
        ],
        compiler_params=params(0),
    )(
        features,
        dw,
        branch_weight,
        jnp.broadcast_to(col_sum[None], (8, channels)),
        pool_weight,
        proj_weight,
    )
    pooled = pooled8[0]
    pool_pre = pool_pre8[0]
    proj_all = projs.transpose(1, 0, 2, 3).reshape(5, hold, hold)
    proj_main = proj_all[:4].reshape(4 * hold, hold)

    branch_out = jnp.maximum(pre, 0.0).astype(BF16)
    pool_out = jnp.maximum(pool_pre, 0.0).astype(BF16)
    pool_term = jnp.sum(pool_out.astype(F32)[:, None] * proj_all[4].astype(F32), axis=0)
    mixed = jnp.dot(branch_out, proj_main, preferred_element_type=F32) + pool_term[None, :]
    hidden = jnp.maximum(mixed, 0.0).astype(BF16)
    logits = jnp.einsum("pc,ck->kp", hidden, class_weight, preferred_element_type=F32)
    expo = jnp.exp(logits)
    soft = expo / jnp.sum(expo, axis=0, keepdims=True)
    label_row = lax.dynamic_slice_in_dim(labels.reshape(-1), me_g * own, own)
    onehot = (lax.broadcasted_iota(jnp.int32, (classes, own), 0) == label_row[None, :]).astype(F32)
    valid = (label_row < classes).astype(F32)
    grad_logit = ((soft - onehot) * valid[None, :] / math.sqrt(total_pixels)).astype(BF16)
    class_part = jnp.einsum("pc,kp->kc", hidden, grad_logit, preferred_element_type=F32)
    back_hidden = jnp.einsum("ck,kp->pc", class_weight, grad_logit, preferred_element_type=F32)
    grad_mixed = (back_hidden * (mixed > 0)).astype(BF16)
    col_part = jnp.sum(grad_mixed.astype(F32), axis=0)
    back_pre = jnp.einsum("pd,cd->pc", grad_mixed, proj_main, preferred_element_type=F32)
    grad_pre = (back_pre * (pre > 0)).astype(BF16)
    proj_part = jnp.einsum("pc,pd->cd", branch_out, grad_mixed, preferred_element_type=F32)
    proj_part = (
        proj_part.reshape(4, 4, own_hold, hold).transpose(1, 0, 2, 3).reshape(4, hold, hold)
    )
    small_rows = -(-(classes + 1) // 8) * 8
    small = jnp.concatenate(
        [class_part, col_part[None], jnp.zeros((small_rows - classes - 1, hold), F32)], axis=0
    )

    halves = channels // 256
    depth_lines = 32
    span = halves * hold // n_rows
    rest_used = halves * depth_lines + hold + small_rows
    rest_span = -(-rest_used // (n_rows * 16)) * 16
    branch_full, rest_full = pl.pallas_call(
        functools.partial(backward_kernel, n_rows),
        out_shape=(
            jax.ShapeDtypeStruct((4, n_rows, span, 256), F32),
            jax.ShapeDtypeStruct((n_rows, rest_span, 256), F32),
        ),
        in_specs=[vspec()] * 6,
        out_specs=(vspec(),) * 2,
        scratch_shapes=[
            pltpu.VMEM((4, 4, hold, own), BF16),
            pltpu.VMEM((3, 3 * hold, channels), F32),
            pltpu.VMEM((depth_lines, channels), F32),
            pltpu.VMEM((4, n_rows, span, 256), BF16),
            pltpu.VMEM((n_rows, rest_span, 256), BF16),
            pltpu.VMEM((4, n_rows, span, 256), BF16),
            pltpu.VMEM((n_rows, rest_span, 256), BF16),
            pltpu.VMEM((4, span, 256), BF16),
            pltpu.VMEM((rest_span, 256), BF16),
            pltpu.VMEM((4, n_rows, span, 256), BF16),
            pltpu.VMEM((n_rows, rest_span, 256), BF16),
            pltpu.VMEM((4, hold, hold), F32),
            pltpu.VMEM((4, small_rows, hold), F32),
            dma(12),
            dma(12),
            dma(3),
            dma(3),
            dma(3),
            dma(3),
            dma(5 * (n_rows - 1)),
            dma(5 * (n_rows - 1)),
            dma(5 * (n_rows - 1)),
            dma(5 * (n_rows - 1)),
        ],
        compiler_params=params(1),
    )(
        grad_pre.T.reshape(4, hold, own),
        proj_part,
        small,
        padded,
        dw,
        branch_weight[1:].transpose(0, 2, 1),
    )
    grad_branch = (
        branch_full.reshape(4, halves, hold, 256).transpose(0, 1, 3, 2).reshape(4, channels, hold)
    )
    rest = rest_full.reshape(n_rows * rest_span, 256)
    at = halves * depth_lines
    grad_depth = (
        rest[:at]
        .reshape(halves, depth_lines, 256)
        .transpose(1, 0, 2)
        .reshape(depth_lines, channels)[:27]
        .reshape(3, 3, 3, channels)
    )
    proj_main_grad = rest[at : at + hold].reshape(4, own_hold, hold)
    at += hold
    grad_class = rest[at : at + classes].T
    col_total = rest[at + classes]
    back_pool = jnp.sum(proj_all[4].astype(F32) * col_total[None, :], axis=1)
    grad_poolpre = (back_pool * (pool_pre > 0)).astype(BF16)
    grad_pool = pooled[:, None] * grad_poolpre.astype(F32)[None, :]
    own_pool = lax.dynamic_slice_in_dim(pool_out, me_g * own_hold, own_hold)
    pool_proj = own_pool.astype(F32)[:, None] * col_total[None, :]
    grad_proj = jnp.concatenate([proj_main_grad, pool_proj[None]], axis=0)
    return (grad_branch, grad_depth, grad_pool, grad_proj, grad_class)


def solution(mesh):
    return jax.shard_map(
        per_device,
        mesh=mesh,
        in_specs=(
            P("rows", None, "grp"),
            P(None, None, None, "grp"),
            P(None, "grp", None),
            P("grp", None),
            P(None, "grp", None),
            P(),
            P("rows", None),
        ),
        out_specs=(
            P(None, "grp", None),
            P(None, None, None, "grp"),
            P("grp", None),
            P(None, "grp", None),
            P(),
        ),
        check_vma=False,
    )
```

```python
import functools
import math

import jax
import jax.numpy as jnp
from jax import lax
from jax.experimental import pallas as pl
from jax.experimental.pallas import tpu as pltpu
from jax.sharding import PartitionSpec as P

RATES = (6, 12, 18)
MARGIN = 18
MESH = pl.DeviceIdType.MESH
F32 = jnp.float32
BF16 = jnp.bfloat16
VMEM_LIMIT = 56 * 1024 * 1024


def vspec():
    return pl.BlockSpec(memory_space=pltpu.VMEM)


def remote(src, dst, send, recv, rows_at, grp_at):
    return pltpu.make_async_remote_copy(
        src_ref=src,
        dst_ref=dst,
        send_sem=send,
        recv_sem=recv,
        device_id=(rows_at, grp_at),
        device_id_type=MESH,
    )


def greet(places):
    barrier = pltpu.get_barrier_semaphore()
    for place in places:
        pl.semaphore_signal(barrier, inc=1, device_id=place, device_id_type=MESH)
    pl.semaphore_wait(barrier, len(places))


def places_of(n_rows, n_grp, me_r, me_g):
    row_peers = [(lax.rem(me_r + j, n_rows), me_g) for j in range(1, n_rows)]
    grp_peers = [(me_r, lax.rem(me_g + j, n_grp)) for j in range(1, n_grp)]
    return row_peers, grp_peers


def forward_kernel(
    n_rows,
    total_pixels,
    features,
    dw,
    weight,
    pool_weight,
    proj,
    pre_out,
    f,
    proj_out,
    pool_out,
    pooled_out,
    dep,
    cross,
    to_mate,
    from_mate,
    to_x,
    from_x,
    col_sum,
    sums,
    parts,
    projs,
    local_sem,
    halo_send,
    halo_recv,
    mate_send,
    mate_recv,
    x_send,
    x_recv,
    sum_send,
    sum_recv,
    part_send,
    part_recv,
    proj_send,
    proj_recv,
):
    me_r, me_g = lax.axis_index("rows"), lax.axis_index("grp")
    row_peers, grp_peers = places_of(n_rows, 4, me_r, me_g)
    height = f.shape[0] - 2 * MARGIN
    width = f.shape[1]
    channels = f.shape[2]
    hold = weight.shape[2]
    quarter_rows = height // 4
    mate = me_g + 1 - 2 * lax.rem(me_g, 2)
    x_peer = lax.rem(me_g + 2, 4)
    diag = lax.rem(mate + 2, 4)
    greet(row_peers + grp_peers)

    after, before = lax.rem(me_r + 1, n_rows), lax.rem(me_r + n_rows - 1, n_rows)
    piece = MARGIN // 3
    up, down = [], []
    for t in range(3):
        up.append(
            remote(
                features.at[pl.ds(height - piece * (t + 1), piece)],
                f.at[pl.ds(MARGIN - piece * (t + 1), piece)],
                halo_send.at[t],
                halo_recv.at[t],
                after,
                me_g,
            )
        )
        down.append(
            remote(
                features.at[pl.ds(piece * t, piece)],
                f.at[pl.ds(MARGIN + height + piece * t, piece)],
                halo_send.at[3 + t],
                halo_recv.at[3 + t],
                before,
                me_g,
            )
        )
    middle = pltpu.make_async_copy(features, f.at[pl.ds(MARGIN, height)], local_sem)
    middle.start()
    for t in range(3):

        @pl.when(me_r < n_rows - 1)
        def _():
            up[t].start()

        @pl.when(me_r > 0)
        def _():
            down[t].start()

    @pl.when(me_r == 0)
    def _():
        f[pl.ds(0, MARGIN)] = jnp.zeros((MARGIN, width, channels), BF16)

    @pl.when(me_r == n_rows - 1)
    def _():
        f[pl.ds(MARGIN + height, MARGIN)] = jnp.zeros((MARGIN, width, channels), BF16)

    projs[me_g] = proj[...]
    proj_copies = []
    for j, (pr, pg) in enumerate(grp_peers):
        copy = remote(proj, projs.at[me_g], proj_send.at[j], proj_recv.at[j], pr, pg)
        copy.start()
        proj_copies.append(copy)

    column = lax.broadcasted_iota(jnp.int32, (width, 128), 0)

    def quarter(q, k, put):
        def pair(p, carry):
            first_row = q * quarter_rows + p * 2 + MARGIN
            if k == 0:
                lhs = f[pl.ds(first_row, 2)].reshape(2 * width, channels)
            else:
                rate = RATES[k - 1]

                def chunk(cc, inner):
                    ch = pl.ds(pl.multiple_of(cc * 128, 128), 128)
                    for i in range(2):
                        h = first_row + i
                        taps = [f[h + (a - 1) * rate, :, ch].astype(F32) for a in range(3)]
                        sides = []
                        for b in range(3):
                            gains = [dw[k - 1, a, b : b + 1, ch] for a in range(3)]
                            sides.append(
                                gains[0] * taps[0] + gains[1] * taps[1] + gains[2] * taps[2]
                            )
                        left = jnp.where(column >= rate, pltpu.roll(sides[0], rate, 0), 0.0)
                        right = jnp.where(
                            column < width - rate, pltpu.roll(sides[2], width - rate, 0), 0.0
                        )
                        dep[i * width : (i + 1) * width, ch] = (left + sides[1] + right).astype(
                            BF16
                        )
                    return inner

                lax.fori_loop(0, channels // 128, chunk, 0)
                lhs = dep[...]
            at_row = pl.ds(pl.multiple_of(p * 2 * width, 2 * width), 2 * width)
            put(at_row, jnp.dot(lhs, weight[k], preferred_element_type=F32))
            return carry

        lax.fori_loop(0, quarter_rows // 2, pair, 0)

    seconds, crossings = [], []

    def branch(k):
        def put_mate(slot):
            def put(at_row, value):
                to_mate[k, slot, at_row] = value.astype(BF16)

            return put

        def put_cross(at_row, value):
            cross[at_row] = value

        def put_own(at_row, value):
            pre_out[at_row, k * hold : (k + 1) * hold] = value

        def to_core(slot):
            copy = remote(
                to_mate.at[k, slot],
                from_mate.at[k, slot],
                mate_send.at[2 * k + slot],
                mate_recv.at[2 * k + slot],
                me_r,
                mate,
            )
            copy.start()
            return copy

        quarter(diag, k, put_mate(0))
        first = to_core(0)
        quarter(x_peer, k, put_cross)
        first.wait()
        to_x[k] = (cross[...] + from_mate[k, 0].astype(F32)).astype(BF16)
        crossing = remote(
            to_x.at[k], from_x.at[k], x_send.at[k], x_recv.at[k], me_r, x_peer
        )
        crossing.start()
        crossings.append(crossing)
        quarter(mate, k, put_mate(1))
        seconds.append(to_core(1))
        quarter(me_g, k, put_own)

    middle.wait()

    def add_row(h, held):
        row = f[MARGIN + h].astype(F32)
        return held + jnp.sum(row.reshape(width // 8, 8, channels), axis=0)

    held = lax.fori_loop(0, height, add_row, jnp.zeros((8, channels), F32))
    col_sum[...] = jnp.broadcast_to(jnp.sum(held, axis=0, keepdims=True), (8, channels))
    sums[me_r] = col_sum[...]
    sum_copies = []
    for j, (pr, pg) in enumerate(row_peers):
        copy = remote(col_sum, sums.at[me_r], sum_send.at[j], sum_recv.at[j], pr, pg)
        copy.start()
        sum_copies.append(copy)
    branch(0)
    for copy in sum_copies:
        copy.wait()
    pooled = sums[0]
    for j in range(1, n_rows):
        pooled = pooled + sums[j]
    pooled = pooled / total_pixels
    pooled_out[...] = pooled
    parts[me_g] = jnp.dot(
        pooled,
        pool_weight[...].astype(F32),
        precision=lax.Precision.HIGHEST,
        preferred_element_type=F32,
    )
    part_copies = []
    for j, (pr, pg) in enumerate(grp_peers):
        copy = remote(
            parts.at[me_g], parts.at[me_g], part_send.at[j], part_recv.at[j], pr, pg
        )
        copy.start()
        part_copies.append(copy)
    for copy in part_copies:
        copy.wait()
    pool_out[...] = parts[0] + parts[1] + parts[2] + parts[3]
    for copy in proj_copies:
        copy.wait()
    proj_out[...] = projs[...]

    for k in range(1, 4):

        @pl.when(me_r > 0)
        def _():
            up[k - 1].wait_recv()

        @pl.when(me_r < n_rows - 1)
        def _():
            down[k - 1].wait_recv()

        branch(k)

    for k in range(4):
        seconds[k].wait()
        crossings[k].wait()
        span = slice(k * hold, (k + 1) * hold)
        pre_out[:, span] = (
            pre_out[:, span] + from_mate[k, 1].astype(F32) + from_x[k].astype(F32)
        )
    for t in range(3):

        @pl.when(me_r < n_rows - 1)
        def _():
            up[t].wait_send()

        @pl.when(me_r > 0)
        def _():
            down[t].wait_send()


def backward_kernel(
    n_rows,
    grad,
    proj,
    small,
    f,
    dw,
    weight_t,
    branch_out,
    rest_out,
    grads,
    acc,
    depth,
    terms,
    rest,
    landed,
    landed_rest,
    total,
    total_rest,
    gathered,
    gathered_rest,
    proj_slots,
    small_slots,
    big_send,
    big_recv,
    proj_send,
    proj_recv,
    small_send,
    small_recv,
    s_send,
    s_recv,
    g_send,
    g_recv,
):
    me_r, me_g = lax.axis_index("rows"), lax.axis_index("grp")
    row_peers, grp_peers = places_of(n_rows, 4, me_r, me_g)
    greet(row_peers + grp_peers)
    mate = me_g + 1 - 2 * lax.rem(me_g, 2)
    x_peer = lax.rem(me_g + 2, 4)
    height = f.shape[0] - 2 * MARGIN
    width, channels = f.shape[1], f.shape[2]
    hold = grad.shape[1]
    own = grad.shape[2]
    halves = channels // 256

    crossing, near = [], []
    for k in range(4):
        one = remote(
            grad.at[k], grads.at[me_g, k], big_send.at[k], big_recv.at[k], me_r, x_peer
        )
        two = remote(
            grad.at[k], grads.at[me_g, k], big_send.at[4 + k], big_recv.at[4 + k], me_r, mate
        )
        one.start()
        two.start()
        crossing.append(one)
        near.append(two)
    others = []
    for j, (pr, pg) in enumerate(grp_peers):
        one = remote(proj.at[pg], proj_slots.at[me_g], proj_send.at[j], proj_recv.at[j], pr, pg)
        two = remote(small, small_slots.at[me_g], small_send.at[j], small_recv.at[j], pr, pg)
        one.start()
        two.start()
        others += [one, two]
    proj_slots[me_g] = proj[me_g]
    small_slots[me_g] = small[...]
    grads[me_g] = grad[...]
    depth[...] = jnp.zeros(depth.shape, F32)
    lane = lax.broadcasted_iota(jnp.int32, (hold, width), 1)
    pairs = own // (2 * width)

    def products(k):
        acc[...] = jnp.zeros(acc.shape, F32)

        def step(p, carry):
            q, within = p // pairs, lax.rem(p, pairs)
            at = pl.ds(pl.multiple_of(within * 2 * width, 2 * width), 2 * width)
            block = grads[q, k, :, at]
            if k == 0:
                rows = f[pl.ds(p * 2 + MARGIN, 2)].reshape(2 * width, channels)
                acc[0, :hold] += jnp.dot(block, rows, preferred_element_type=F32)
                return carry
            rate = RATES[k - 1]
            wide = block.astype(F32)
            lefts, rights = [], []
            for i in range(2):
                x = wide[:, i * width : (i + 1) * width]
                lefts.append(
                    jnp.where(lane < width - rate, pltpu.roll(x, width - rate, 1), 0.0)
                )
                rights.append(jnp.where(lane >= rate, pltpu.roll(x, rate, 1), 0.0))
            left = jnp.concatenate(lefts, axis=1).astype(BF16)
            right = jnp.concatenate(rights, axis=1).astype(BF16)
            for a in range(3):
                rows = f[pl.ds(p * 2 + MARGIN + (a - 1) * rate, 2)].reshape(2 * width, channels)
                for b, lhs in enumerate((left, block, right)):
                    acc[a, b * hold : (b + 1) * hold] += jnp.dot(
                        lhs, rows, preferred_element_type=F32
                    )
            return carry

        lax.fori_loop(0, height // 2, step, 0)

    def spread(unit, source, target):
        copies = []
        for j, (pr, pg) in enumerate(row_peers):
            at = unit * (n_rows - 1) + j
            copy = remote(source(pr), target, s_send.at[at], s_recv.at[at], pr, pg)
            copy.start()
            copies.append(copy)
        return copies

    def share(unit, source, target):
        copies = []
        for j, (pr, pg) in enumerate(row_peers):
            at = unit * (n_rows - 1) + j
            copy = remote(source, target, g_send.at[at], g_recv.at[at], pr, pg)
            copy.start()
            copies.append(copy)
        return copies

    def add_up(parts):
        value = parts[0].astype(F32)
        for j in range(1, n_rows):
            value = value + parts[j].astype(F32)
        return value.astype(BF16)

    spreading, sharing = [], []

    def finish(k):
        for copy in spreading[k]:
            copy.wait()
        total[k] = add_up([landed[k, j] for j in range(n_rows)])
        gathered[k, me_r] = total[k]
        sharing.append(share(k, total.at[k], gathered.at[k, me_r]))

    span = terms.shape[2]
    passing = []
    for k in range(4):
        crossing[k].wait()
        copy = remote(
            grads.at[x_peer, k],
            grads.at[x_peer, k],
            big_send.at[8 + k],
            big_recv.at[8 + k],
            me_r,
            mate,
        )
        copy.start()
        passing.append(copy)
        near[k].wait()
        copy.wait()
        products(k)
        if k == 0:
            value = acc[0, :hold]
        else:
            value = jnp.zeros((hold, channels), F32)
            for a in range(3):
                for b in range(3):
                    at = (k - 1) * 9 + a * 3 + b
                    term = acc[a, b * hold : (b + 1) * hold]
                    value = value + dw[k - 1, a, b : b + 1, :] * term
                    depth[at : at + 1, :] = jnp.sum(
                        weight_t[k - 1].astype(F32) * term, axis=0, keepdims=True
                    )
        flat = jnp.concatenate(
            [value[:, c * 256 : (c + 1) * 256] for c in range(halves)], axis=0
        ).astype(BF16)
        terms[k] = flat.reshape(n_rows, span, 256)
        landed[k, me_r] = terms[k, me_r]
        spreading.append(
            spread(k, lambda pr, k=k: terms.at[k, pr], landed.at[k, me_r])
        )
        if k > 0:
            finish(k - 1)

    for copy in others:
        copy.wait()
    lines = [depth[:, c * 256 : (c + 1) * 256] for c in range(halves)]
    lines.append(proj_slots[0] + proj_slots[1] + proj_slots[2] + proj_slots[3])
    lines.append(small_slots[0] + small_slots[1] + small_slots[2] + small_slots[3])
    flat = jnp.concatenate(lines, axis=0)
    spare = rest.shape[0] * rest.shape[1] - flat.shape[0]
    flat = jnp.concatenate([flat, jnp.zeros((spare, 256), F32)], axis=0).astype(BF16)
    rest[...] = flat.reshape(rest.shape)
    landed_rest[me_r] = rest[me_r]
    last = spread(4, lambda pr: rest.at[pr], landed_rest.at[me_r])
    finish(3)
    for copy in last:
        copy.wait()
    total_rest[...] = add_up([landed_rest[j] for j in range(n_rows)])
    gathered_rest[me_r] = total_rest[...]
    last = share(4, total_rest, gathered_rest.at[me_r])
    for k in range(4):
        for copy in sharing[k]:
            copy.wait()
        branch_out[k] = gathered[k].astype(F32)
    for copy in last:
        copy.wait()
    rest_out[...] = gathered_rest[...].astype(F32)


def params(number):
    return pltpu.CompilerParams(
        collective_id=number, has_side_effects=True, vmem_limit_bytes=VMEM_LIMIT
    )


def dma(count):
    return pltpu.SemaphoreType.DMA((count,))


def per_device(
    features, depth_weight, branch_weight, pool_weight, proj_weight, class_weight, labels
):
    height, width, channels = features.shape
    n_rows = lax.axis_size("rows")
    me_g = lax.axis_index("grp")
    hold = branch_weight.shape[2]
    own_hold = proj_weight.shape[1]
    classes = class_weight.shape[1]
    total_pixels = height * n_rows * width
    own = height * width // 4
    dw = depth_weight

    pre, padded, projs, pool_pre8, pooled8 = pl.pallas_call(
        functools.partial(forward_kernel, n_rows, total_pixels),
        out_shape=(
            jax.ShapeDtypeStruct((own, 4 * hold), F32),
            jax.ShapeDtypeStruct((height + 2 * MARGIN, width, channels), BF16),
            jax.ShapeDtypeStruct((4,) + proj_weight.shape, BF16),
            jax.ShapeDtypeStruct((8, hold), F32),
            jax.ShapeDtypeStruct((8, channels), F32),
        ),
        in_specs=[pl.BlockSpec(memory_space=pl.ANY)] + [vspec()] * 4,
        out_specs=(vspec(),) * 5,
        scratch_shapes=[
            pltpu.VMEM((2 * width, channels), BF16),
            pltpu.VMEM((own, hold), F32),
            pltpu.VMEM((4, 2, own, hold), BF16),
            pltpu.VMEM((4, 2, own, hold), BF16),
            pltpu.VMEM((4, own, hold), BF16),
            pltpu.VMEM((4, own, hold), BF16),
            pltpu.VMEM((8, channels), F32),
            pltpu.VMEM((n_rows, 8, channels), F32),
            pltpu.VMEM((4, 8, hold), F32),
            pltpu.VMEM((4,) + proj_weight.shape, BF16),
            pltpu.SemaphoreType.DMA,
            dma(6),
            dma(6),
            dma(8),
            dma(8),
            dma(4),
            dma(4),
            dma(n_rows - 1),
            dma(n_rows - 1),
            dma(3),
            dma(3),
            dma(3),
            dma(3),
        ],
        compiler_params=params(0),
    )(
        features,
        dw,
        branch_weight,
        pool_weight,
        proj_weight,
    )
    pooled = pooled8[0]
    pool_pre = pool_pre8[0]
    proj_all = projs.transpose(1, 0, 2, 3).reshape(5, hold, hold)
    proj_main = proj_all[:4].reshape(4 * hold, hold)

    branch_out = jnp.maximum(pre, 0.0).astype(BF16)
    pool_out = jnp.maximum(pool_pre, 0.0).astype(BF16)
    pool_term = jnp.sum(pool_out.astype(F32)[:, None] * proj_all[4].astype(F32), axis=0)
    mixed = jnp.dot(branch_out, proj_main, preferred_element_type=F32) + pool_term[None, :]
    hidden = jnp.maximum(mixed, 0.0).astype(BF16)
    logits = jnp.einsum("pc,ck->kp", hidden, class_weight, preferred_element_type=F32)
    expo = jnp.exp(logits)
    soft = expo / jnp.sum(expo, axis=0, keepdims=True)
    label_row = lax.dynamic_slice_in_dim(labels.reshape(-1), me_g * own, own)
    onehot = (lax.broadcasted_iota(jnp.int32, (classes, own), 0) == label_row[None, :]).astype(F32)
    valid = (label_row < classes).astype(F32)
    grad_logit = ((soft - onehot) * valid[None, :] / math.sqrt(total_pixels)).astype(BF16)
    class_part = jnp.einsum("pc,kp->kc", hidden, grad_logit, preferred_element_type=F32)
    back_hidden = jnp.einsum("ck,kp->pc", class_weight, grad_logit, preferred_element_type=F32)
    grad_mixed = (back_hidden * (mixed > 0)).astype(BF16)
    col_part = jnp.sum(grad_mixed.astype(F32), axis=0)
    back_pre = jnp.einsum("pd,cd->pc", grad_mixed, proj_main, preferred_element_type=F32)
    grad_pre = (back_pre * (pre > 0)).astype(BF16)
    proj_part = jnp.einsum("pc,pd->cd", branch_out, grad_mixed, preferred_element_type=F32)
    proj_part = (
        proj_part.reshape(4, 4, own_hold, hold).transpose(1, 0, 2, 3).reshape(4, hold, hold)
    )
    small_rows = -(-(classes + 1) // 8) * 8
    small = jnp.concatenate(
        [class_part, col_part[None], jnp.zeros((small_rows - classes - 1, hold), F32)], axis=0
    )

    halves = channels // 256
    depth_lines = 32
    span = halves * hold // n_rows
    rest_used = halves * depth_lines + hold + small_rows
    rest_span = -(-rest_used // (n_rows * 16)) * 16
    branch_full, rest_full = pl.pallas_call(
        functools.partial(backward_kernel, n_rows),
        out_shape=(
            jax.ShapeDtypeStruct((4, n_rows, span, 256), F32),
            jax.ShapeDtypeStruct((n_rows, rest_span, 256), F32),
        ),
        in_specs=[vspec()] * 6,
        out_specs=(vspec(),) * 2,
        scratch_shapes=[
            pltpu.VMEM((4, 4, hold, own), BF16),
            pltpu.VMEM((3, 3 * hold, channels), F32),
            pltpu.VMEM((depth_lines, channels), F32),
            pltpu.VMEM((4, n_rows, span, 256), BF16),
            pltpu.VMEM((n_rows, rest_span, 256), BF16),
            pltpu.VMEM((4, n_rows, span, 256), BF16),
            pltpu.VMEM((n_rows, rest_span, 256), BF16),
            pltpu.VMEM((4, span, 256), BF16),
            pltpu.VMEM((rest_span, 256), BF16),
            pltpu.VMEM((4, n_rows, span, 256), BF16),
            pltpu.VMEM((n_rows, rest_span, 256), BF16),
            pltpu.VMEM((4, hold, hold), F32),
            pltpu.VMEM((4, small_rows, hold), F32),
            dma(12),
            dma(12),
            dma(3),
            dma(3),
            dma(3),
            dma(3),
            dma(5 * (n_rows - 1)),
            dma(5 * (n_rows - 1)),
            dma(5 * (n_rows - 1)),
            dma(5 * (n_rows - 1)),
        ],
        compiler_params=params(1),
    )(
        grad_pre.T.reshape(4, hold, own),
        proj_part,
        small,
        padded,
        dw,
        branch_weight[1:].transpose(0, 2, 1),
    )
    grad_branch = (
        branch_full.reshape(4, halves, hold, 256).transpose(0, 1, 3, 2).reshape(4, channels, hold)
    )
    rest = rest_full.reshape(n_rows * rest_span, 256)
    at = halves * depth_lines
    grad_depth = (
        rest[:at]
        .reshape(halves, depth_lines, 256)
        .transpose(1, 0, 2)
        .reshape(depth_lines, channels)[:27]
        .reshape(3, 3, 3, channels)
    )
    proj_main_grad = rest[at : at + hold].reshape(4, own_hold, hold)
    at += hold
    grad_class = rest[at : at + classes].T
    col_total = rest[at + classes]
    back_pool = jnp.sum(proj_all[4].astype(F32) * col_total[None, :], axis=1)
    grad_poolpre = (back_pool * (pool_pre > 0)).astype(BF16)
    grad_pool = pooled[:, None] * grad_poolpre.astype(F32)[None, :]
    own_pool = lax.dynamic_slice_in_dim(pool_out, me_g * own_hold, own_hold)
    pool_proj = own_pool.astype(F32)[:, None] * col_total[None, :]
    grad_proj = jnp.concatenate([proj_main_grad, pool_proj[None]], axis=0)
    return (grad_branch, grad_depth, grad_pool, grad_proj, grad_class)


def solution(mesh):
    return jax.shard_map(
        per_device,
        mesh=mesh,
        in_specs=(
            P("rows", None, "grp"),
            P(None, None, None, "grp"),
            P(None, "grp", None),
            P("grp", None),
            P(None, "grp", None),
            P(),
            P("rows", None),
        ),
        out_specs=(
            P(None, "grp", None),
            P(None, None, None, "grp"),
            P("grp", None),
            P(None, "grp", None),
            P(),
        ),
        check_vma=False,
    )
```
